32 devices in a mesh: dp: 4 (over y, core), row: 4 (over z), col: 2 (over x).
Axes of the slice: x: 2, y: 2, z: 4, core: 2. Of those that a mesh axis runs over, the one named last changes fastest.
Arguments:
- tokens: bfloat16 [4096, 6144], P(('dp', 'col'), 'row'), may hold values from -6 to 6
- weight_in: bfloat16 [6144, 12288], P('row', 'col'), may hold values from -0.078125 to 0.078125
- weight_out: bfloat16 [12288, 6144], P('col', 'row'), may hold values from -0.0546875 to 0.0546875
- cotangent: bfloat16 [4096, 6144], P(('dp', 'col'), 'row'), may hold values from -1.5 to 1.5
Outputs:
- input_grad: bfloat16 [4096, 6144], P(('dp', 'col'), 'row')
- weight_in_grad: bfloat16 [6144, 12288], P('row', ('col', 'dp'))
- weight_out_grad: bfloat16 [12288, 6144], P(('col', 'dp'), 'row')
The draws below stay inside these ranges and needn't reach their ends.
All inputs are finite; a program needn't handle non-finite values.
Results may differ from the reference program's by a relative error of at most 0.0051.
Values may be sent and summed in bfloat16 or wider, within the bound.
A program may use at most 320 MiB of HBM per device.

```python
import math
import jax
import jax.numpy as jnp

D = 6144
FF = 12288
TOKENS = 4096


def steps_of(rng, shape, split, smallest, largest):
    level, own = 1.0, jax.random.fold_in(rng, 6)
    for position, parts in split:
        steps = jnp.exp(jax.random.uniform(jax.random.fold_in(own, position), (parts,), jnp.float32, smallest / len(split), largest / len(split)))
        level = level * jnp.repeat(steps, shape[position] // parts).reshape([-1 if axis == position else 1 for axis in range(len(shape))])
    return level


def gaussian(own_key, dims, spread, reach, split=(), kind=jnp.bfloat16):
    level = steps_of(own_key, dims, split, -0.22, 0.18) if split else 1.0
    entries = jax.random.normal(own_key, dims, jnp.float32) * spread * level
    return jnp.minimum(jnp.maximum(entries, -reach), reach).astype(kind)


def setup_inputs(seed: int = 0) -> dict:
    streams_of = jax.random.split(jax.random.key(seed), 5)
    tokens = gaussian(streams_of[0], (TOKENS, D), 1.0, 6.0, ((0, 8), (1, 4)))
    weight_in = gaussian(streams_of[1], (D, FF), D ** -0.5, 0.078125, ((0, 4), (1, 2)))
    weight_out = gaussian(streams_of[2], (FF, D), FF ** -0.5, 0.0546875, ((0, 2), (1, 4)))
    cotangent = gaussian(streams_of[3], (TOKENS, D), 0.25, 1.5, ((0, 8), (1, 4)))
    return {"tokens": tokens, "weight_in": weight_in, "weight_out": weight_out, "cotangent": cotangent}


def gelu_exact(values):
    return 0.5 * values * (1.0 + jax.scipy.special.erf(values / math.sqrt(2.0)))

def gelu_slope(values):
    cumulative = 0.5 * (1.0 + jax.scipy.special.erf(values / math.sqrt(2.0)))
    density = jnp.exp(-0.5 * values * values) / math.sqrt(2.0 * math.pi)
    return cumulative + values * density

def reference(tokens, weight_in, weight_out, cotangent):
    preact = jnp.dot(tokens, weight_in, preferred_element_type=jnp.float32)
    activated = gelu_exact(preact).astype(jnp.bfloat16)
    grad_hidden = jnp.dot(cotangent, weight_out.T, preferred_element_type=jnp.float32)
    grad_preact = (grad_hidden * gelu_slope(preact)).astype(jnp.bfloat16)
    weight_in_grad = jnp.dot(tokens.T, grad_preact, preferred_element_type=jnp.float32).astype(jnp.bfloat16)
    weight_out_grad = jnp.dot(activated.T, cotangent, preferred_element_type=jnp.float32).astype(jnp.bfloat16)
    input_grad = jnp.dot(grad_preact, weight_in.T, preferred_element_type=jnp.float32).astype(jnp.bfloat16)
    return (input_grad, weight_in_grad, weight_out_grad)
```

```python
import math

import jax
import jax.numpy as jnp
from jax import lax
from jax.sharding import PartitionSpec as P


def gelu_exact(values):
    return 0.5 * values * (1.0 + jax.scipy.special.erf(values / math.sqrt(2.0)))


def gelu_slope(values):
    cumulative = 0.5 * (1.0 + jax.scipy.special.erf(values / math.sqrt(2.0)))
    density = jnp.exp(-0.5 * values * values) / math.sqrt(2.0 * math.pi)
    return cumulative + values * density


def contract_last(left, right):
    return lax.dot_general(
        left, right, (((1,), (1,)), ((), ())), preferred_element_type=jnp.float32
    )


def contract_first(left, right):
    return lax.dot_general(
        left, right, (((0,), (0,)), ((), ())), preferred_element_type=jnp.float32
    )


def wide(value):
    return value.astype(jnp.float32)


def narrow(value):
    return value.astype(jnp.bfloat16)


def shards(n_dp, n_row, n_col, tokens, weight_in, weight_out, cotangent):
    rows = tokens.shape[0]
    hidden = weight_in.shape[1]
    part = hidden // n_dp
    width = 256 if part % 256 == 0 else 128
    dp = lax.axis_index("dp")

    def gather(block):
        blocks = [block]
        for shift in range(1, n_col):
            pairs = [(i, (i - shift) % n_col) for i in range(n_col)]
            blocks.append(lax.ppermute(block, "col", pairs))
        return jnp.concatenate(blocks, axis=0)

    tok_all, cot_all = gather(tokens), gather(cotangent)

    slots, bits = [0], []
    bit = n_dp // 2
    while bit:
        slots = slots + [s ^ bit for s in slots]
        bits.insert(0, bit)
        bit //= 2

    row = lax.axis_index("row")

    class Line:
        def __init__(self, units):
            self.units, self.own, self.right, self.left = units, {}, {}, {}
            self.steps = units + n_row - 2

        def pick(self, held, first, sign):
            cases = [held.get(first + sign * z) for z in range(n_row)]
            some = next(c for c in cases if c is not None)
            return wide(lax.select_n(row, *[some if c is None else c for c in cases]))

        def step(self, t):
            right = self.pick(self.own, t, -1)
            left = self.pick(self.own, t - (n_row - 1), 1)
            if t:
                right = right + wide(self.right[t - 1])
                left = left + wide(self.left[t - 1])
            up = [(z, z + 1) for z in range(n_row - 1)]
            down = [(z + 1, z) for z in range(n_row - 1)]
            self.right[t] = lax.ppermute(narrow(right), "row", up)
            self.left[t] = lax.ppermute(narrow(left), "row", down)

        def total(self, c):
            right = self.pick({k: v for k, v in self.right.items() if k >= c}, c - 1, 1)
            left = self.pick({k: v for k, v in self.left.items() if k >= c}, c + n_row - 2, -1)
            zero = jnp.zeros((), jnp.float32)
            return (
                self.own[c]
                + jnp.where(row > 0, right, zero)
                + jnp.where(row < n_row - 1, left, zero)
            )

    def exchange(keep, send, bit):
        pairs = [(i, i ^ bit) for i in range(n_dp)]
        return keep + wide(lax.ppermute(narrow(send), "dp", pairs))

    def replica_sum(total, axis):
        for bit in bits:
            half = total.shape[axis] // 2
            keep = lax.slice_in_dim(total, 0, half, axis=axis)
            send = lax.slice_in_dim(total, half, 2 * half, axis=axis)
            total = exchange(keep, send, bit)
        return narrow(total)

    starts = list(range(0, part, width))
    halves = 2
    units = len(starts) * halves
    half = tok_all.shape[0] // halves
    forward, backward = Line(units), Line(units)
    acts, slopes = {}, {}
    in_grads, out_grads, input_total = [], [], None
    weights = {}

    def load(k):
        places = [(dp ^ s) * part + starts[k] for s in slots]
        weights[k] = (
            jnp.concatenate(
                [lax.dynamic_slice_in_dim(weight_in, p, width, axis=1) for p in places], axis=1
            ),
            jnp.concatenate(
                [lax.dynamic_slice_in_dim(weight_out, p, width, axis=0) for p in places], axis=0
            ),
        )

    def block(array, h):
        return array[h * half : (h + 1) * half]

    def ready_forward(c):
        if c < units:
            if c // halves not in weights:
                load(c // halves)
            rows_in = block(tok_all, c % halves)
            forward.own[c] = jnp.dot(
                rows_in, weights[c // halves][0], preferred_element_type=jnp.float32
            )

    def ready_backward(c):
        if c < units:
            backward.own[c] = contract_last(block(cot_all, c % halves), weights[c // halves][1])

    def fence(line, t, work):
        if t:
            line.right[t - 1], line.left[t - 1], work = lax.optimization_barrier(
                (line.right[t - 1], line.left[t - 1], work)
            )
        return work

    ready_forward(0)
    ready_backward(0)
    for t in range(forward.steps + 1):
        c = t - (n_row - 1)
        fresh = forward.own.get(t)
        fresh = fence(forward, t, fresh)
        if fresh is not None:
            forward.own[t] = fresh
        if t < forward.steps:
            forward.step(t)
        ready_forward(t + 1)
        fresh = backward.own.get(t)
        fresh = fence(backward, t, (fresh, forward.own.get(t + 1)))
        if fresh[0] is not None:
            backward.own[t] = fresh[0]
        if fresh[1] is not None:
            forward.own[t + 1] = fresh[1]
        if t < backward.steps:
            backward.step(t)
        ready_backward(t + 1)
        if c < 0:
            continue
        preact, grad_hidden = forward.total(c), backward.total(c)
        acts[c] = narrow(gelu_exact(preact))
        slopes[c] = narrow(grad_hidden * gelu_slope(preact))
        if c % halves == halves - 1:
            k = c // halves
            mine = range(k * halves, (k + 1) * halves)
            activated = jnp.concatenate([acts[i] for i in mine], axis=0)
            grad_preact = jnp.concatenate([slopes[i] for i in mine], axis=0)
            in_grads.append(replica_sum(contract_first(tok_all, grad_preact), 1))
            out_grads.append(replica_sum(contract_first(activated, cot_all), 0))
            term = contract_last(grad_preact, weights[k][0])
            input_total = term if input_total is None else input_total + term

    input_grad = input_total[:rows]
    for shift in range(1, n_col):
        pairs = [(i, (i + shift) % n_col) for i in range(n_col)]
        piece = narrow(input_total[shift * rows : (shift + 1) * rows])
        input_grad = input_grad + wide(lax.ppermute(piece, "col", pairs))
    return (
        narrow(input_grad),
        jnp.concatenate(in_grads, axis=1),
        jnp.concatenate(out_grads, axis=0),
    )


def solution(mesh):
    sizes = [mesh.shape[name] for name in ("dp", "row", "col")]

    def body(*arrays):
        return shards(*sizes, *arrays)

    return jax.shard_map(
        body,
        mesh=mesh,
        in_specs=(
            P(("dp", "col"), "row"),
            P("row", "col"),
            P("col", "row"),
            P(("dp", "col"), "row"),
        ),
        out_specs=(P(("dp", "col"), "row"), P("row", ("col", "dp")), P(("col", "dp"), "row")),
        check_vma=False,
    )
```

```python
import math

import jax
import jax.numpy as jnp
from jax import lax
from jax.sharding import PartitionSpec as P


def gelu_exact(values):
    return 0.5 * values * (1.0 + jax.scipy.special.erf(values / math.sqrt(2.0)))


def gelu_slope(values):
    cumulative = 0.5 * (1.0 + jax.scipy.special.erf(values / math.sqrt(2.0)))
    density = jnp.exp(-0.5 * values * values) / math.sqrt(2.0 * math.pi)
    return cumulative + values * density


def contract_last(left, right):
    return lax.dot_general(
        left, right, (((1,), (1,)), ((), ())), preferred_element_type=jnp.float32
    )


def contract_first(left, right):
    return lax.dot_general(
        left, right, (((0,), (0,)), ((), ())), preferred_element_type=jnp.float32
    )


def wide(value):
    return value.astype(jnp.float32)


def narrow(value):
    return value.astype(jnp.bfloat16)


def shards(n_dp, n_row, n_col, tokens, weight_in, weight_out, cotangent):
    rows = tokens.shape[0]
    hidden = weight_in.shape[1]
    part = hidden // n_dp
    width = 256 if part % 256 == 0 else 128
    dp = lax.axis_index("dp")

    def gather(block):
        blocks = [block]
        for shift in range(1, n_col):
            pairs = [(i, (i - shift) % n_col) for i in range(n_col)]
            blocks.append(lax.ppermute(block, "col", pairs))
        return blocks

    halves = 2
    group = max(n_col // halves, 1)

    def whole(blocks):
        return jnp.concatenate(blocks, axis=0) if len(blocks) > 1 else blocks[0]

    def parts_of(blocks):
        return [whole(blocks[i * group : (i + 1) * group]) for i in range(halves)]

    tok_blocks, cot_blocks = gather(tokens), gather(cotangent)
    tok_parts, cot_parts = parts_of(tok_blocks), parts_of(cot_blocks)
    tok_all, cot_all = whole(tok_parts), whole(cot_parts)

    slots, bits = [0], []
    bit = n_dp // 2
    while bit:
        slots = slots + [s ^ bit for s in slots]
        bits.insert(0, bit)
        bit //= 2

    row = lax.axis_index("row")

    class Line:
        def __init__(self, units):
            self.units, self.own, self.right, self.left = units, {}, {}, {}
            self.steps = units + n_row - 2

        def pick(self, held, first, sign):
            cases = [held.get(first + sign * z) for z in range(n_row)]
            some = next(c for c in cases if c is not None)
            return wide(lax.select_n(row, *[some if c is None else c for c in cases]))

        def sums(self, t):
            right = self.pick(self.own, t, -1)
            left = self.pick(self.own, t - (n_row - 1), 1)
            if t:
                right = right + wide(self.right[t - 1])
                left = left + wide(self.left[t - 1])
            return narrow(right), narrow(left)

        def send(self, t, right, left):
            up = [(z, z + 1) for z in range(n_row - 1)]
            down = [(z + 1, z) for z in range(n_row - 1)]
            self.right[t] = lax.ppermute(right, "row", up)
            self.left[t] = lax.ppermute(left, "row", down)

        def total(self, c):
            right = self.pick({k: v for k, v in self.right.items() if k >= c}, c - 1, 1)
            left = self.pick({k: v for k, v in self.left.items() if k >= c}, c + n_row - 2, -1)
            zero = jnp.zeros((), jnp.float32)
            return (
                self.own[c]
                + jnp.where(row > 0, right, zero)
                + jnp.where(row < n_row - 1, left, zero)
            )

    def exchange(keep, send, bit):
        pairs = [(i, i ^ bit) for i in range(n_dp)]
        return keep + wide(lax.ppermute(narrow(send), "dp", pairs))

    def replica_sum(product, size, axis):
        total = None
        for bit in bits:
            half = size // 2
            if total is None:
                keep, send = product(0, half), product(half, size)
            else:
                keep = lax.slice_in_dim(total, 0, half, axis=axis)
                send = lax.slice_in_dim(total, half, size, axis=axis)
            total, size = exchange(keep, send, bit), half
        return narrow(product(0, size) if total is None else total)

    starts = list(range(0, part, width))
    units = len(starts) * halves
    forward, backward = Line(units), Line(units)
    acts, slopes = {}, {}
    in_grads, out_grads, input_total = [], [], None
    w_in, w_out = {}, {}

    def ready_forward(c, place):
        k, h = c // halves, c % halves
        if h == 0:
            places = [(place ^ s) * part + starts[k] for s in slots]
            w_in[k] = jnp.concatenate(
                [lax.dynamic_slice_in_dim(weight_in, p, width, axis=1) for p in places], axis=1
            )
        forward.own[c] = jnp.dot(tok_parts[h], w_in[k], preferred_element_type=jnp.float32)

    def ready_backward(c, place):
        k, h = c // halves, c % halves
        if h == 0:
            places = [(place ^ s) * part + starts[k] for s in slots]
            w_out[k] = jnp.concatenate(
                [lax.dynamic_slice_in_dim(weight_out, p, width, axis=0) for p in places], axis=0
            )
        backward.own[c] = contract_last(cot_parts[h], w_out[k])

    def turn(line, t, place, other_sends):
        held = (line.own.get(t), line.right.get(t - 1), line.left.get(t - 1))
        held, place, other_sends = lax.optimization_barrier((held, place, other_sends))
        for table, key, value in zip(
            (line.own, line.right, line.left), (t, t - 1, t - 1), held
        ):
            if value is not None:
                table[key] = value
        return place

    ready_forward(0, dp)
    ready_backward(0, dp)
    place, sent = dp, None
    for t in range(forward.steps + 1):
        c = t - (n_row - 1)
        place = turn(forward, t, place, sent)
        sent = None
        if t < forward.steps:
            sent = forward.sums(t)
            forward.send(t, *sent)
        if t + 1 < units:
            ready_forward(t + 1, place)
        place = turn(backward, t, place, sent)
        sent = None
        if t < backward.steps:
            sent = backward.sums(t)
            backward.send(t, *sent)
        if t + 1 < units:
            ready_backward(t + 1, place)
        if c < 0:
            continue
        preact, grad_hidden = forward.total(c), backward.total(c)
        acts[c] = narrow(gelu_exact(preact))
        slopes[c] = narrow(grad_hidden * gelu_slope(preact))
        if c % halves == halves - 1:
            k = c // halves
            mine = range(k * halves, (k + 1) * halves)
            activated = jnp.concatenate([acts[i] for i in mine], axis=0)
            grad_preact = jnp.concatenate([slopes[i] for i in mine], axis=0)
            size = grad_preact.shape[1]

            def in_term(a, b):
                return contract_first(tok_all, grad_preact[:, a:b])

            def out_term(a, b):
                return contract_first(activated[:, a:b], cot_all)

            in_grads.append(replica_sum(in_term, size, 1))
            out_grads.append(replica_sum(out_term, size, 0))
            term = contract_last(grad_preact, w_in[k])
            input_total = term if input_total is None else input_total + term

    input_grad = input_total[:rows]
    for shift in range(1, n_col):
        pairs = [(i, (i + shift) % n_col) for i in range(n_col)]
        piece = narrow(input_total[shift * rows : (shift + 1) * rows])
        input_grad = input_grad + wide(lax.ppermute(piece, "col", pairs))
    return (
        narrow(input_grad),
        jnp.concatenate(in_grads, axis=1),
        jnp.concatenate(out_grads, axis=0),
    )


def solution(mesh):
    sizes = [mesh.shape[name] for name in ("dp", "row", "col")]

    def body(*arrays):
        return shards(*sizes, *arrays)

    return jax.shard_map(
        body,
        mesh=mesh,
        in_specs=(
            P(("dp", "col"), "row"),
            P("row", "col"),
            P("col", "row"),
            P(("dp", "col"), "row"),
        ),
        out_specs=(P(("dp", "col"), "row"), P("row", ("col", "dp")), P(("col", "dp"), "row")),
        check_vma=False,
    )
```
